32 devices in a mesh: wave: 4 (over y, x), slab: 8 (over z, core).
Axes of the slice: x: 2, y: 2, z: 4, core: 2. Of those that a mesh axis runs over, the one named last changes fastest.
Arguments:
- levels: int32 [2048, 2048], P('slab', 'wave'), may hold values from 0 to 15
- offsets: float32 [2048, 2048], P('slab', 'wave'), may hold values from -0.3 to 0.3
- targets: int32 [4, 64, 2], replicated, may hold values from 0 to 2047
- w_in: float32 [256], replicated, may hold values from -96 to 96
- b_in: float32 [256], replicated, may hold values from -87 to 87
- w_out: bfloat16 [256, 8], replicated, may hold values from -0.046875 to 0.046875
- b_out: float32 [8], replicated, may hold values from -2 to 2
Outputs:
- width_gradient: float32 [2048, 2048], P('slab', 'wave')
The draws below stay inside these ranges and needn't reach their ends.
All inputs are finite; a program needn't handle non-finite values.
Results may differ from the reference program's by a relative error of at most 0.0039.
Values may be sent and summed in bfloat16 or wider, within the bound.
A program may use at most 64 MiB of HBM per device.

```python
import math
import jax
import jax.numpy as jnp
from jax import lax

N = 2048
UNITS = 256
SPOTS = 64
LEVELS = 16
WAVES = 4
FOCAL = 128
SPOT_LEVEL = 256


def pillar_units(key, slope_low, slope_high, place_low, place_high):
    sign_key, size_key, place_key = jax.random.split(jax.random.fold_in(key, 11), 3)
    signs = jnp.where(jax.random.bernoulli(sign_key, 0.5, (UNITS,)), 1.0, -1.0).astype(jnp.float32)
    fraction = jax.random.uniform(size_key, (UNITS,), jnp.float32, 0.0, 1.0)
    magnitude = slope_low * jnp.exp(fraction * math.log(slope_high / slope_low))
    places = jax.random.uniform(place_key, (UNITS,), jnp.float32, place_low, place_high)
    slopes = signs * magnitude
    return (slopes, -slopes * places)


def draw_w_in(key, part):
    slopes, biases = pillar_units(key, 32.0, 96.0, 0.1, 0.9)
    return slopes


def draw_b_in(key, part):
    slopes, biases = pillar_units(key, 32.0, 96.0, 0.1, 0.9)
    return biases


def place_ends(array, rng, least, high):
    longest = array.shape.index(max(array.shape))
    spots = []
    for shift in (0, 1):
        where = [jax.random.randint(jax.random.fold_in(rng, axis), (), 0, length) for axis, length in enumerate(array.shape)]
        where[longest] = (where[longest] + shift) % array.shape[longest]
        spots.append(tuple(where))
    return array.at[spots[0]].set(least).at[spots[1]].set(high)


def steps_of(rng, extent, cuts, low, largest):
    level = 1.0
    for dim, parts in cuts:
        steps = jax.random.uniform(jax.random.fold_in(jax.random.fold_in(rng, 6), dim), (parts,), jnp.float32, low / len(cuts), largest / len(cuts))
        level = level * jnp.repeat(jnp.exp(steps), extent[dim] // parts).reshape((-1,) + (1,) * (len(extent) - 1 - dim))
    return level


def noise(key, dims, spread, limit, cuts=(), held_as=jnp.bfloat16):
    array = jax.random.normal(key, dims, jnp.float32) * spread
    if len(cuts) > 0:
        array = steps_of(key, dims, cuts, -0.22, 0.18) * array
    return jnp.clip(array, min=-limit, max=limit).astype(held_as)


def setup_inputs(seed: int = 0) -> dict:
    seeds = jax.random.split(jax.random.key(seed), 8)
    return {
        "levels": place_ends(jax.random.randint(seeds[0], (N, N), 0, LEVELS), jax.random.fold_in(seeds[0], 1), 0, LEVELS - 1).astype(jnp.int32),
        "offsets": noise(seeds[1], (N, N), 0.1, 0.3, ((0, 8), (1, 4)), jnp.float32),
        "targets": place_ends(jax.random.randint(seeds[2], (WAVES, SPOTS, 2), 0, N), jax.random.fold_in(seeds[2], 1), 0, N - 1).astype(jnp.int32),
        "w_in": draw_w_in(jax.random.fold_in(seeds[7], 71), 0),
        "b_in": draw_b_in(jax.random.fold_in(seeds[7], 71), 0),
        "w_out": noise(seeds[5], (UNITS, 2 * WAVES), (UNITS * 64) ** -0.5, 0.046875),
        "b_out": noise(seeds[6], (2 * WAVES,), 0.5, 2.0, (), jnp.float32),
    }


def level_widths(levels, offsets):
    return 0.3 + levels.astype(jnp.float32) * (0.4 / (LEVELS - 1)) + offsets

def surrogate(widths, w_in, b_in, w_out, b_out):
    pre_act = widths[..., None] * w_in + b_in
    hidden = (pre_act * jax.nn.sigmoid(pre_act)).astype(jnp.bfloat16)
    mixed_out = jnp.einsum('rch,hj->jrc', hidden.astype(jnp.float32), w_out.astype(jnp.float32))
    return (mixed_out + b_out[:, None, None]).astype(jnp.bfloat16)

def width_slope(widths, w_in, b_in, w_out, cotangent):
    pre_act = widths[..., None] * w_in + b_in
    sigmoid_value = jax.nn.sigmoid(pre_act)
    back_hidden = jnp.einsum('jrc,hj->rch', cotangent.astype(jnp.float32), w_out.astype(jnp.float32))
    act_slope = sigmoid_value * (1.0 + pre_act * (1.0 - sigmoid_value))
    return lax.optimization_barrier(jnp.sum(back_hidden * act_slope * w_in, axis=-1))

def frequencies(length, first_index, total_len):
    index_all = first_index + jnp.arange(length, dtype=jnp.int32)
    signed_index = jnp.where(index_all < total_len // 2, index_all, index_all - total_len)
    return signed_index.astype(jnp.float32) * (2.0 * math.pi / total_len)

def transfer(wavelength, kx_rows, ky_cols, focal_length):
    wave_number = 2.0 * math.pi / wavelength
    kz_square = wave_number * wave_number - kx_rows[:, None] ** 2 - ky_cols[None, :] ** 2
    kz_root = jnp.sqrt(jnp.abs(kz_square))
    is_open = kz_square > 0.0
    phase_angle = jnp.where(is_open, focal_length * kz_root, 0.0)
    amplitude = jnp.where(is_open, 1.0, jnp.exp(-focal_length * kz_root))
    return (amplitude * jnp.cos(phase_angle), amplitude * jnp.sin(phase_angle))

def reference(levels, offsets, targets, w_in, b_in, w_out, b_out):
    block_rows = min(N, 64)
    count_blocks = N // block_rows
    widths = level_widths(levels, offsets)

    def forward_block(width_rows):
        return surrogate(width_rows, w_in, b_in, w_out, b_out)
    transmission = lax.map(forward_block, widths.reshape(count_blocks, block_rows, N))
    transmission = jnp.transpose(transmission, (1, 0, 2, 3)).reshape(2 * WAVES, N, N)
    kx_all = frequencies(N, 0, N)

    def per_wave(wave_index):
        wavelength = 1.5 + wave_index.astype(jnp.float32) / (WAVES - 1)
        kern_re, kern_im = transfer(wavelength, kx_all, kx_all, float(FOCAL))
        kernel = lax.complex(kern_re, kern_im)
        source = lax.complex(transmission[wave_index].astype(jnp.float32), transmission[WAVES + wave_index].astype(jnp.float32))
        focal_field = jnp.fft.ifft2(kernel * jnp.fft.fft2(source))
        intensity = focal_field.real ** 2 + focal_field.imag ** 2
        own_targets = targets[wave_index]
        spot_map = jnp.zeros((N, N), jnp.float32).at[own_targets[:, 0], own_targets[:, 1]].add(float(SPOT_LEVEL))
        adjoint = (intensity - spot_map) * focal_field / WAVES
        back_field = jnp.fft.ifft2(jnp.conj(kernel) * jnp.fft.fft2(adjoint))
        return jnp.stack([back_field.real, back_field.imag]).astype(jnp.bfloat16)
    cotangent = lax.map(per_wave, jnp.arange(WAVES, dtype=jnp.int32))
    cotangent = jnp.transpose(cotangent, (1, 0, 2, 3)).reshape(2 * WAVES, count_blocks, block_rows, N)
    cotangent = jnp.transpose(cotangent, (1, 0, 2, 3))

    def backward_block(pieces):
        return width_slope(pieces[0], w_in, b_in, w_out, pieces[1])
    gradient = lax.map(backward_block, (widths.reshape(count_blocks, block_rows, N), cotangent))
    return gradient.reshape(N, N)
```

```python
import math

import jax
import jax.numpy as jnp
import ml_dtypes
import numpy as np
from jax import lax
from jax.experimental import pallas as pl
from jax.experimental.pallas import tpu as pltpu
from jax.sharding import Mesh, PartitionSpec as P

LEVELS = 16
RADIX = 8
ROWS = 16
GRANT = 58 * 1024 * 1024
GROUP = ("wave", "duo")
SLAB = ("zed", "duo")


def params(**more):
    return pltpu.CompilerParams(vmem_limit_bytes=GRANT, **more)


def split16(table):
    high = table.astype(np.float32).astype(ml_dtypes.bfloat16)
    low = (table - high.astype(np.float64)).astype(np.float32).astype(ml_dtypes.bfloat16)
    return high, low


def dft_block(points):
    index = np.arange(points)
    angle = -2.0 * np.pi * ((index[:, None] * index[None, :]) % points) / points
    re, im = np.cos(angle), np.sin(angle)
    return split16(np.block([[re, -im], [im, re]]))


def twiddles(points):
    angle = -2.0 * np.pi * np.outer(np.arange(RADIX), np.arange(points)) / (RADIX * points)
    return np.stack([np.cos(angle), np.sin(angle)]).astype(np.float32)


def add(a, b):
    return (a[0] + b[0], a[1] + b[1])


def sub(a, b):
    return (a[0] - b[0], a[1] - b[1])


def turn(a, sign):
    return (-a[1], a[0]) if sign > 0 else (a[1], -a[0])


def dft4(x, sign):
    a, b = add(x[0], x[2]), sub(x[0], x[2])
    c, d = add(x[1], x[3]), turn(sub(x[1], x[3]), sign)
    return [add(a, c), add(b, d), sub(a, c), sub(b, d)]


def dft8(x, sign):
    even, odd = dft4(x[0::2], sign), dft4(x[1::2], sign)
    half = math.sqrt(0.5)
    one = add(odd[1], turn(odd[1], sign))
    three = sub(turn(odd[3], sign), odd[3])
    odd = [odd[0], (one[0] * half, one[1] * half), turn(odd[2], sign), (three[0] * half, three[1] * half)]
    return [add(e, o) for e, o in zip(even, odd)] + [sub(e, o) for e, o in zip(even, odd)]


def mul(a, b):
    return (a[0] * b[0] - a[1] * b[1], a[0] * b[1] + a[1] * b[0])


def mul_conj(a, b):
    return (a[0] * b[0] + a[1] * b[1], a[1] * b[0] - a[0] * b[1])


def dot(a, b):
    return jnp.dot(a, b, preferred_element_type=jnp.float32)


def halves(x):
    high = x.astype(jnp.bfloat16)
    return high, (x - high.astype(jnp.float32)).astype(jnp.bfloat16)


FULL = 32000.0
LOG2 = math.log(2.0)


def send_rows(rows, coded):
    return 2 * rows + (ROWS if coded else 0)


def put_block(out_ref, k, y):
    rows, lanes = y.shape
    if out_ref.dtype != jnp.int16:
        out_ref[k] = y
        return
    largest = jnp.maximum(jnp.max(jnp.abs(y), axis=0, keepdims=True), 1e-30)
    power = jnp.ceil(jnp.log(largest) * (1.0 / LOG2) + 0.001)
    factor = FULL / jnp.exp(power * LOG2)
    out_ref[k, :rows] = jnp.round(y * factor).astype(jnp.int32).astype(jnp.int16)
    out_ref[k, rows:] = jnp.broadcast_to(power, (ROWS, lanes)).astype(jnp.int32).astype(jnp.int16)


def block_scale(in_ref, k):
    if in_ref.dtype != jnp.int16:
        return None
    power = in_ref[k, in_ref.shape[1] - ROWS :].astype(jnp.int32).astype(jnp.float32)
    return jnp.exp(power * LOG2) * (1.0 / FULL)


def as_float(x):
    return x.astype(jnp.int32).astype(jnp.float32) if x.dtype == jnp.int16 else x


def width_of(levels_ref, offsets_ref):
    return 0.3 + levels_ref[...].astype(jnp.float32) * (0.4 / (LEVELS - 1)) + offsets_ref[...]


def surrogate_kernel(levels_ref, offsets_ref, slope_ref, bias_ref, out_w_ref, out_b_ref, t_ref, width_s, mix_s):
    waves, duo, parts, rows, cols = t_ref.shape
    width_s[...] = width_of(levels_ref, offsets_ref)
    units = slope_ref.shape[0]
    lane = slope_ref.shape[1]
    count = width_s.shape[1] // lane
    for r in range(rows):
        for c in range(count):
            w = jnp.broadcast_to(width_s[r : r + 1, c * lane : (c + 1) * lane], (units, lane))
            y = w * slope_ref[...] + bias_ref[...]
            hidden = (y * jnp.tanh(y) + y).astype(jnp.bfloat16)
            mixed = dot(out_w_ref[...], hidden)[: waves * parts] + out_b_ref[...]
            mix_s[:, r, c * lane : (c + 1) * lane] = mixed
    for wave in range(waves):
        for d in range(duo):
            for part in range(parts):
                t_ref[wave, d, part] = mix_s[wave * parts + part, :, d * cols : (d + 1) * cols].astype(jnp.bfloat16)


def slope_kernel(levels_ref, offsets_ref, slope_ref, bias_ref, back_w_ref, cot_ref, grad_ref, width_s, mix_s):
    waves, duo, parts, rows, cols = cot_ref.shape
    width_s[...] = width_of(levels_ref, offsets_ref)
    units = slope_ref.shape[0]
    lane = slope_ref.shape[1]
    count = width_s.shape[1] // lane
    js = waves * parts
    for r in range(rows):
        for c in range(count):
            w = jnp.broadcast_to(width_s[r : r + 1, c * lane : (c + 1) * lane], (units, lane))
            y = w * slope_ref[...] + bias_ref[...]
            th = jnp.tanh(y)
            act = ((1.0 + th) * (1.0 + (y - y * th))).astype(jnp.bfloat16)
            mixed = dot(back_w_ref[...], act)
            mix_s[:, r, c * lane : (c + 1) * lane] = mixed[:js] + mixed[js : 2 * js]
    for d in range(duo):
        at = slice(d * cols, (d + 1) * cols)
        total = jnp.zeros((rows, cols), jnp.float32)
        for wave in range(waves):
            for part in range(parts):
                total = total + mix_s[wave * parts + part, :, at] * cot_ref[wave, d, part].astype(jnp.float32)
        grad_ref[:, at] = total


def unit_tables(w_in, b_in, lane):
    units = w_in.shape[0]
    spread = lambda x: jnp.broadcast_to((0.5 * x)[:, None], (units, lane))
    return spread(w_in), spread(b_in)


def whole(shape):
    return pl.BlockSpec(shape, lambda i: (0,) * len(shape))


def surrogate(levels, offsets, w_in, b_in, w_out, b_out, waves, duo):
    rows, cols = levels.shape
    parts = 2
    js = waves * parts
    units = w_in.shape[0]
    lane = min(256, cols)
    slope, bias = unit_tables(w_in, b_in, lane)
    ordered = w_out.reshape(units, parts, waves).transpose(2, 1, 0).reshape(js, units)
    pad = max(16, js)
    ordered = jnp.zeros((pad, units), jnp.bfloat16).at[:js].set(ordered)
    biases = b_out.reshape(parts, waves).T.reshape(js, 1)
    shape = (waves, duo, parts, rows, cols // duo)
    strip = pl.BlockSpec((ROWS, cols), lambda i: (i, 0))
    return pl.pallas_call(
        surrogate_kernel,
        grid=(rows // ROWS,),
        in_specs=[strip, strip, whole(slope.shape), whole(bias.shape), whole(ordered.shape), whole(biases.shape)],
        out_specs=pl.BlockSpec(shape[:3] + (ROWS, cols // duo), lambda i: (0, 0, 0, i, 0)),
        out_shape=jax.ShapeDtypeStruct(shape, jnp.bfloat16),
        scratch_shapes=[pltpu.VMEM((ROWS, cols), jnp.float32), pltpu.VMEM((js, ROWS, cols), jnp.float32)],
        compiler_params=params(),
        name="surrogate",
    )(levels, offsets, slope, bias, ordered, biases)


def width_slope(levels, offsets, w_in, b_in, w_out, cot):
    rows, cols = levels.shape
    waves, duo, parts = cot.shape[:3]
    js = waves * parts
    units = w_in.shape[0]
    lane = min(256, cols)
    slope, bias = unit_tables(w_in, b_in, lane)
    ordered = w_out.astype(jnp.float32).reshape(units, parts, waves).transpose(2, 1, 0).reshape(js, units)
    high, low = halves(ordered * (0.5 * w_in)[None, :])
    weights = jnp.concatenate([high, low])
    strip = pl.BlockSpec((ROWS, cols), lambda i: (i, 0))
    return pl.pallas_call(
        slope_kernel,
        grid=(rows // ROWS,),
        in_specs=[
            strip,
            strip,
            whole(slope.shape),
            whole(bias.shape),
            whole(weights.shape),
            pl.BlockSpec(cot.shape[:3] + (ROWS, cols // duo), lambda i: (0, 0, 0, i, 0)),
        ],
        out_specs=strip,
        out_shape=jax.ShapeDtypeStruct((rows, cols), jnp.float32),
        scratch_shapes=[pltpu.VMEM((ROWS, cols), jnp.float32), pltpu.VMEM((js, ROWS, cols), jnp.float32)],
        compiler_params=params(),
        name="width_slope",
    )(levels, offsets, slope, bias, weights, cot)


def col_forward_chunks(load, tw_ref, hi_s, lo_s):
    points, cols = hi_s.shape[1] // 2, hi_s.shape[2]
    lane = tw_ref.shape[3]

    def chunk(i, _):
        row = pl.multiple_of(i * ROWS, ROWS)
        at = pl.ds(row, ROWS)
        at_im = pl.ds(pl.multiple_of(points + row, ROWS), ROWS)
        for c in range(cols // lane):
            lanes = slice(c * lane, (c + 1) * lane)
            out = dft8([load(n, at, lanes) for n in range(RADIX)], -1)
            for k in range(RADIX):
                pair = out[k] if k == 0 else mul(out[k], (tw_ref[0, k, at, :], tw_ref[1, k, at, :]))
                hi_s[k, at, lanes], lo_s[k, at, lanes] = halves(pair[0])
                hi_s[k, at_im, lanes], lo_s[k, at_im, lanes] = halves(pair[1])
        return 0

    lax.fori_loop(0, points // ROWS, chunk, 0)


def col_forward_dots(fh_ref, fl_ref, hi_s, lo_s, out_ref):
    points = hi_s.shape[1] // 2

    def step(k, _):
        high = hi_s[k]
        y = dot(fh_ref[...], high) + dot(fh_ref[...], lo_s[k]) + dot(fl_ref[...], high)
        put_block(out_ref, k, y)
        return 0

    lax.fori_loop(0, RADIX, step, 0)


def col_inverse_dots(in_ref, gh_ref, gl_ref, tw_ref, mid_s):
    points, cols = mid_s.shape[2], mid_s.shape[3]
    lane = tw_ref.shape[3]
    scale = 1.0 / (RADIX * points)

    def step(k, _):
        high, low = halves(as_float(in_ref[k, : 2 * points]))
        z = dot(gh_ref[...], high) + dot(gh_ref[...], low) + dot(gl_ref[...], high)
        sent = block_scale(in_ref, k)
        z = z * (scale if sent is None else sent[:1] * scale)
        for c in range(cols // lane):
            lanes = slice(c * lane, (c + 1) * lane)
            pair = mul_conj((z[:points, lanes], z[points:, lanes]), (tw_ref[0, k], tw_ref[1, k]))
            mid_s[k, 0, :, lanes] = pair[0]
            mid_s[k, 1, :, lanes] = pair[1]
        return 0

    lax.fori_loop(0, RADIX, step, 0)


def first_kernel(t_ref, tw_ref, fh_ref, fl_ref, out_ref, hi_s, lo_s):
    def load(n, at, lanes):
        return (t_ref[n, 0, at, lanes].astype(jnp.float32), t_ref[n, 1, at, lanes].astype(jnp.float32))

    col_forward_chunks(load, tw_ref, hi_s, lo_s)
    col_forward_dots(fh_ref, fl_ref, hi_s, lo_s, out_ref)


def focus_kernel(level, waves, in_ref, tw_ref, fh_ref, fl_ref, gh_ref, gl_ref, rowsel_ref, colsel_ref, out_ref, hi_s, lo_s, mid_s, spot_s):
    points, cols = mid_s.shape[2], mid_s.shape[3]
    lane = tw_ref.shape[3]
    col_inverse_dots(in_ref, gh_ref, gl_ref, tw_ref, mid_s)
    for n in range(RADIX):
        spot_s[n] = dot(rowsel_ref[n], colsel_ref[...]) * level

    def chunk(i, _):
        at = pl.ds(pl.multiple_of(i * ROWS, ROWS), ROWS)
        for c in range(cols // lane):
            lanes = slice(c * lane, (c + 1) * lane)
            out = dft8([(mid_s[k, 0, at, lanes], mid_s[k, 1, at, lanes]) for k in range(RADIX)], 1)
            for n in range(RADIX):
                re, im = out[n]
                weight = (re * re + im * im - spot_s[n, at, lanes]) * (1.0 / waves)
                mid_s[n, 0, at, lanes] = weight * re
                mid_s[n, 1, at, lanes] = weight * im
        return 0

    lax.fori_loop(0, points // ROWS, chunk, 0)

    def load(n, at, lanes):
        return (mid_s[n, 0, at, lanes], mid_s[n, 1, at, lanes])

    col_forward_chunks(load, tw_ref, hi_s, lo_s)
    col_forward_dots(fh_ref, fl_ref, hi_s, lo_s, out_ref)


def last_kernel(in_ref, tw_ref, gh_ref, gl_ref, out_ref, mid_s):
    points, cols = mid_s.shape[2], mid_s.shape[3]
    lane = tw_ref.shape[3]
    col_inverse_dots(in_ref, gh_ref, gl_ref, tw_ref, mid_s)

    def chunk(i, _):
        at = pl.ds(pl.multiple_of(i * ROWS, ROWS), ROWS)
        for c in range(cols // lane):
            lanes = slice(c * lane, (c + 1) * lane)
            out = dft8([(mid_s[k, 0, at, lanes], mid_s[k, 1, at, lanes]) for k in range(RADIX)], 1)
            for n in range(RADIX):
                out_ref[n, 0, at, lanes] = out[n][0].astype(jnp.bfloat16)
                out_ref[n, 1, at, lanes] = out[n][1].astype(jnp.bfloat16)
        return 0

    lax.fori_loop(0, points // ROWS, chunk, 0)


def filter_kernel(conjugate, in_ref, kern_ref, tw_ref, fh_ref, fl_ref, gh_ref, gl_ref, out_ref, hi_s, lo_s, mid_s, sent_s):
    rows, points = mid_s.shape[2], mid_s.shape[3]
    lane = 128
    scale = 1.0 / (RADIX * points)
    coded = in_ref.dtype == jnp.int16
    if coded:
        for n in range(RADIX):
            sent_s[n] = block_scale(in_ref, n)

    def load(n, at, lanes):
        x = as_float(in_ref[n, at, lanes])
        return x * sent_s[n, :, lanes] if coded else x

    def forward(i, _):
        at = pl.ds(pl.multiple_of(i * ROWS, ROWS), ROWS)
        at_im = pl.ds(pl.multiple_of(rows + i * ROWS, ROWS), ROWS)
        for c in range(points // lane):
            lanes = slice(c * lane, (c + 1) * lane)
            lanes_im = slice(points + c * lane, points + (c + 1) * lane)
            out = dft8([(load(n, at, lanes), load(n, at_im, lanes)) for n in range(RADIX)], -1)
            for k in range(RADIX):
                pair = out[k] if k == 0 else mul(out[k], (tw_ref[0, k, :, lanes], tw_ref[1, k, :, lanes]))
                hi_s[k, at, lanes], lo_s[k, at, lanes] = halves(pair[0])
                hi_s[k, at, lanes_im], lo_s[k, at, lanes_im] = halves(pair[1])
        return 0

    lax.fori_loop(0, rows // ROWS, forward, 0)
    combine = mul_conj if conjugate else mul

    def step(k, _):
        high = hi_s[k]
        y = dot(high, gh_ref[...]) + dot(lo_s[k], gh_ref[...]) + dot(high, gl_ref[...])
        re, im = combine((y[:, :points], y[:, points:]), (kern_ref[0, k], kern_ref[1, k]))
        re_h, re_l = halves(re)
        im_h, im_l = halves(im)
        high = jnp.concatenate([re_h, im_h], axis=1)
        low = jnp.concatenate([re_l, im_l], axis=1)
        z = dot(high, fh_ref[...]) + dot(low, fh_ref[...]) + dot(high, fl_ref[...])
        z = z * scale
        t_re, t_im = tw_ref[0, k, 0:1, :], tw_ref[1, k, 0:1, :]
        pair = mul_conj((z[:, :points], z[:, points:]), (t_re, t_im))
        mid_s[k, 0] = pair[0]
        mid_s[k, 1] = pair[1]
        return 0

    lax.fori_loop(0, RADIX, step, 0)

    def inverse(i, _):
        at = pl.ds(pl.multiple_of(i * ROWS, ROWS), ROWS)
        for c in range(points // lane):
            lanes = slice(c * lane, (c + 1) * lane)
            out = dft8([(mid_s[k, 0, at, lanes], mid_s[k, 1, at, lanes]) for k in range(RADIX)], 1)
            for n in range(RADIX):
                mid_s[n, 0, at, lanes], mid_s[n, 1, at, lanes] = out[n]
        return 0

    lax.fori_loop(0, rows // ROWS, inverse, 0)

    def send(n, _):
        put_block(out_ref, n, mid_s[n].reshape(2 * rows, points))
        return 0

    lax.fori_loop(0, RADIX, send, 0)


def call(kernel, out_shape, out_type, scratch, name, *args):
    return pl.pallas_call(
        kernel,
        out_shape=jax.ShapeDtypeStruct(out_shape, out_type),
        scratch_shapes=scratch,
        compiler_params=params(),
        name=name,
    )(*args)


def frequencies(index_all, total_len):
    signed_index = jnp.where(index_all < total_len // 2, index_all, index_all - total_len)
    return signed_index.astype(jnp.float32) * (2.0 * math.pi / total_len)


def transfer(wavelength, kx, ky, focal_length):
    wave_number = 2.0 * math.pi / wavelength
    kz_square = wave_number * wave_number - kx**2 - ky**2
    kz_root = jnp.sqrt(jnp.abs(kz_square))
    is_open = kz_square > 0.0
    phase_angle = jnp.where(is_open, focal_length * kz_root, 0.0)
    amplitude = jnp.where(is_open, 1.0, jnp.exp(-focal_length * kz_root))
    return jnp.stack([amplitude * jnp.cos(phase_angle), amplitude * jnp.sin(phase_angle)])


def local(levels, offsets, targets, w_in, b_in, w_out, b_out):
    waves, duo = lax.axis_size("wave"), lax.axis_size("duo")
    slabs, group = waves * duo, waves * duo
    rows_here, cols_here = levels.shape
    length = rows_here * slabs
    points = length // RADIX
    cols = cols_here // duo
    rows = length // group
    own = lax.axis_index("wave") * duo + lax.axis_index("duo")
    wave_index = lax.axis_index("zed")
    wavelength = 1.5 + wave_index.astype(jnp.float32) / (waves - 1)

    def exchange(x, axes):
        return lax.all_to_all(x, axes, split_axis=0, concat_axis=0, tiled=True)

    def regroup(x, blocks):
        if x.shape[0] == blocks:
            return x
        flat = x.transpose(1, 0, 2, 3).reshape(2, blocks, -1, x.shape[3])
        return flat.transpose(1, 0, 2, 3)

    def recolumn(x, blocks):
        if x.shape[0] == blocks:
            return x
        flat = x.transpose(1, 2, 0, 3).reshape(2, x.shape[2], blocks, -1)
        return flat.transpose(2, 0, 1, 3)

    fh, fl = dft_block(points)
    gh, gl = fh.T, fl.T
    fh, fl, gh, gl = (jnp.asarray(np.ascontiguousarray(m)) for m in (fh, fl, gh, gl))
    tw = twiddles(points)
    lane = min(128, cols)
    tw_col = jnp.broadcast_to(jnp.asarray(tw)[:, :, :, None], (2, RADIX, points, lane))
    tw_row = jnp.broadcast_to(jnp.asarray(tw)[:, :, None, :], (2, RADIX, ROWS, points))

    position = own * rows + jnp.arange(rows, dtype=jnp.int32)
    u = position // points + RADIX * (position % points)
    v = jnp.arange(RADIX, dtype=jnp.int32)[:, None] + RADIX * jnp.arange(points, dtype=jnp.int32)[None, :]
    kern = transfer(
        wavelength, frequencies(u, length)[None, :, None], frequencies(v, length)[:, None, :], float(length // 16)
    )

    own_targets = lax.dynamic_index_in_dim(targets, wave_index, 0, keepdims=False)
    rowsel = (jnp.arange(length, dtype=jnp.int32)[:, None] == own_targets[None, :, 0]).astype(jnp.bfloat16)
    rowsel = rowsel.reshape(RADIX, points, -1)
    colsel = (own_targets[:, 1:2] - own * cols == jnp.arange(cols, dtype=jnp.int32)[None, :]).astype(jnp.bfloat16)

    col_shape = (RADIX, 2, points, cols)
    row_shape = (RADIX, 2, rows, points)
    col_pair = [pltpu.VMEM((RADIX, 2 * points, cols), jnp.bfloat16)] * 2
    row_pair = [pltpu.VMEM((RADIX, rows, 2 * points), jnp.bfloat16)] * 2
    coded = group == RADIX
    wire = jnp.int16 if coded else jnp.float32
    col_send = (RADIX, send_rows(points, coded), cols)
    row_send = (RADIX, send_rows(rows, coded), points)

    def to_rows(x):
        if coded:
            return exchange(x, GROUP)
        return recolumn(exchange(regroup(x.reshape(col_shape), group), GROUP), RADIX).reshape(row_send)

    def to_cols(x):
        if coded:
            return exchange(x, GROUP)
        return regroup(exchange(recolumn(x.reshape(row_shape), group), GROUP), RADIX).reshape(col_send)

    def filtered(spectrum, conjugate):
        done = call(
            lambda *refs: filter_kernel(conjugate, *refs),
            row_send,
            wire,
            row_pair + [pltpu.VMEM(row_shape, jnp.float32), pltpu.VMEM((RADIX, ROWS, points), jnp.float32)],
            "filter_back" if conjugate else "filter",
            to_rows(spectrum), kern, tw_row, fh, fl, gh, gl,
        )
        return to_cols(done)

    trans = surrogate(levels, offsets, w_in, b_in, w_out, b_out, waves, duo)
    trans = exchange(trans.reshape((slabs,) + trans.shape[2:]), SLAB)
    spectrum = call(first_kernel, col_send, wire, col_pair, "first", regroup(trans, RADIX), tw_col, fh, fl)
    spectrum = filtered(spectrum, False)
    spectrum = call(
        lambda *refs: focus_kernel(float(length // 8), waves, *refs),
        col_send,
        wire,
        col_pair + [pltpu.VMEM(col_shape, jnp.float32), pltpu.VMEM((RADIX, points, cols), jnp.float32)],
        "focus",
        spectrum, tw_col, fh, fl, gh, gl, rowsel, colsel,
    )
    spectrum = filtered(spectrum, True)
    mid = [pltpu.VMEM(col_shape, jnp.float32)]
    cot = call(last_kernel, col_shape, jnp.bfloat16, mid, "last", spectrum, tw_col, gh, gl)
    cot = exchange(regroup(cot, slabs), SLAB)
    return width_slope(levels, offsets, w_in, b_in, w_out, cot.reshape((waves, duo) + cot.shape[1:]))


def solution(mesh):
    waves, slabs = mesh.shape["wave"], mesh.shape["slab"]
    cut = Mesh(mesh.devices.reshape(waves, waves, slabs // waves), ("wave", "zed", "duo"))
    place = P(("zed", "duo"), "wave")
    placed = (place, place, P(), P(), P(), P(), P())
    return jax.shard_map(local, mesh=cut, in_specs=placed, out_specs=place, check_vma=False)
```

```python
import math

import jax
import jax.numpy as jnp
import ml_dtypes
import numpy as np
from jax import lax
from jax.experimental import pallas as pl
from jax.experimental.pallas import tpu as pltpu
from jax.sharding import Mesh, PartitionSpec as P

LEVELS = 16
RADIX = 8
ROWS = 16
GRANT = 58 * 1024 * 1024
GROUP = ("wave", "duo")
SLAB = ("zed", "duo")


def params(**more):
    return pltpu.CompilerParams(vmem_limit_bytes=GRANT, **more)


def split16(table):
    high = table.astype(np.float32).astype(ml_dtypes.bfloat16)
    low = (table - high.astype(np.float64)).astype(np.float32).astype(ml_dtypes.bfloat16)
    return high, low


def dft_block(points):
    index = np.arange(points)
    angle = -2.0 * np.pi * ((index[:, None] * index[None, :]) % points) / points
    re, im = np.cos(angle), np.sin(angle)
    return split16(np.block([[re, -im], [im, re]]))


def twiddles(points):
    angle = -2.0 * np.pi * np.outer(np.arange(RADIX), np.arange(points)) / (RADIX * points)
    return np.stack([np.cos(angle), np.sin(angle)]).astype(np.float32)


def add(a, b):
    return (a[0] + b[0], a[1] + b[1])


def sub(a, b):
    return (a[0] - b[0], a[1] - b[1])


def turn(a, sign):
    return (-a[1], a[0]) if sign > 0 else (a[1], -a[0])


def dft4(x, sign):
    a, b = add(x[0], x[2]), sub(x[0], x[2])
    c, d = add(x[1], x[3]), turn(sub(x[1], x[3]), sign)
    return [add(a, c), add(b, d), sub(a, c), sub(b, d)]


def dft8(x, sign):
    even, odd = dft4(x[0::2], sign), dft4(x[1::2], sign)
    half = math.sqrt(0.5)
    one = add(odd[1], turn(odd[1], sign))
    three = sub(turn(odd[3], sign), odd[3])
    odd = [odd[0], (one[0] * half, one[1] * half), turn(odd[2], sign), (three[0] * half, three[1] * half)]
    return [add(e, o) for e, o in zip(even, odd)] + [sub(e, o) for e, o in zip(even, odd)]


def mul(a, b):
    return (a[0] * b[0] - a[1] * b[1], a[0] * b[1] + a[1] * b[0])


def mul_conj(a, b):
    return (a[0] * b[0] + a[1] * b[1], a[1] * b[0] - a[0] * b[1])


def dot(a, b):
    return jnp.dot(a, b, preferred_element_type=jnp.float32)


def halves(x):
    high = x.astype(jnp.bfloat16)
    return high, (x - high.astype(jnp.float32)).astype(jnp.bfloat16)


FULL = 32000.0
LOG2 = math.log(2.0)


def send_rows(rows, coded):
    return 2 * rows + (ROWS if coded else 0)


def put_block(out_ref, k, y):
    rows, lanes = y.shape
    if out_ref.dtype != jnp.int16:
        out_ref[k] = y
        return
    largest = jnp.maximum(jnp.max(jnp.abs(y), axis=0, keepdims=True), 1e-30)
    power = jnp.ceil(jnp.log(largest) * (1.0 / LOG2) + 0.001)
    factor = FULL / jnp.exp(power * LOG2)
    out_ref[k, :rows] = jnp.round(y * factor).astype(jnp.int32).astype(jnp.int16)
    out_ref[k, rows:] = jnp.broadcast_to(power, (ROWS, lanes)).astype(jnp.int32).astype(jnp.int16)


def block_scale(in_ref, k):
    if in_ref.dtype != jnp.int16:
        return None
    power = in_ref[k, in_ref.shape[1] - ROWS :].astype(jnp.int32).astype(jnp.float32)
    return jnp.exp(power * LOG2) * (1.0 / FULL)


def as_float(x):
    return x.astype(jnp.int32).astype(jnp.float32) if x.dtype == jnp.int16 else x


class Exchange:
    def __init__(self, axes, count, duo, send_sem, recv_sem, own_sem):
        self.axes, self.count, self.duo = axes, count, duo
        self.send_sem, self.recv_sem, self.own_sem = send_sem, recv_sem, own_sem
        self.me = lax.axis_index(axes[0]) * duo + lax.axis_index(axes[1])

    def other(self, step):
        return lax.rem(self.me + step, self.count)

    def device(self, index):
        return {self.axes[0]: index // self.duo, self.axes[1]: lax.rem(index, self.duo)}

    def enter(self):
        barrier = pltpu.get_barrier_semaphore()
        for step in range(1, self.count):
            pl.semaphore_signal(
                barrier, inc=1, device_id=self.device(self.other(step)), device_id_type=pl.DeviceIdType.MESH
            )
        pl.semaphore_wait(barrier, self.count - 1)

    def copy(self, source, target, step, piece):
        return pltpu.make_async_remote_copy(
            src_ref=source,
            dst_ref=target,
            send_sem=self.send_sem.at[piece, step],
            recv_sem=self.recv_sem.at[piece, step],
            device_id=self.device(self.other(step)),
            device_id_type=pl.DeviceIdType.MESH,
        )

    def own(self, source, target, piece):
        return pltpu.make_async_copy(source, target, self.own_sem.at[piece])


def exchange_scratch(count, pieces):
    return [
        pltpu.SemaphoreType.DMA((pieces, count)),
        pltpu.SemaphoreType.DMA((pieces, count)),
        pltpu.SemaphoreType.DMA((pieces,)),
    ]


PIECES = 4


def send_piece(ex, send_s, out_ref, piece, rows, start):
    at = pl.ds(piece * rows, rows)
    for step in range(1, ex.count):
        copy = ex.copy(send_s.at[ex.other(step), :, at, :], out_ref.at[ex.me, :, at, :], step, piece)
        copy.start() if start else copy.wait()
    copy = ex.own(send_s.at[ex.me, :, at, :], out_ref.at[ex.me, :, at, :], piece)
    copy.start() if start else copy.wait()


def blocks_out(ex, send_s, out_ref, fill, beside):
    if ex is None:
        def plain(k, _):
            fill(k)
            return 0

        lax.fori_loop(0, RADIX, plain, 0)
        beside()
        return

    def step_out(step, _):
        k = ex.other(step)
        fill(k)
        ex.copy(send_s.at[k], out_ref.at[ex.me], step, 0).start()
        return 0

    lax.fori_loop(1, ex.count, step_out, 0)
    fill(ex.me)
    ex.own(send_s.at[ex.me], out_ref.at[ex.me], 0).start()
    beside()
    ex.own(send_s.at[ex.me], out_ref.at[ex.me], 0).wait()

    def step_wait(step, _):
        ex.copy(send_s.at[ex.other(step)], out_ref.at[ex.me], step, 0).wait()
        return 0

    lax.fori_loop(1, ex.count, step_wait, 0)


def strip_widths(levels_ref, offsets_ref, row):
    at = pl.ds(row, ROWS)
    return 0.3 + levels_ref[at, :].astype(jnp.float32) * (0.4 / (LEVELS - 1)) + offsets_ref[at, :]


def each_chunk(widths, slope_ref, bias_ref, body):
    units, lane = slope_ref.shape
    for r in range(ROWS):
        for c in range(widths.shape[1] // lane):
            lanes = slice(c * lane, (c + 1) * lane)
            w = jnp.broadcast_to(widths[r : r + 1, lanes], (units, lane))
            body(r, lanes, w * slope_ref[...] + bias_ref[...])


def mixed_strips(levels_ref, offsets_ref, slope_ref, bias_ref, back_w_ref, mixed_ref, strip_s, first):
    js = mixed_ref.shape[0]

    def strip(i, _):
        widths = strip_widths(levels_ref, offsets_ref, pl.multiple_of((first + i) * ROWS, ROWS))

        def body(r, lanes, y):
            th = jnp.tanh(y)
            act = ((1.0 + th) * (1.0 + (y - y * th))).astype(jnp.bfloat16)
            mixed = dot(back_w_ref[...], act)
            strip_s[:, r, lanes] = mixed[:js] + mixed[js : 2 * js]

        each_chunk(widths, slope_ref, bias_ref, body)
        mixed_ref[:, pl.ds(pl.multiple_of(i * ROWS, ROWS), ROWS), :] = strip_s[...]
        return 0

    lax.fori_loop(0, mixed_ref.shape[1] // ROWS, strip, 0)


def surrogate_kernel(
    make, levels_ref, offsets_ref, slope_ref, bias_ref, back_w_ref, out_w_ref, out_b_ref, out_ref, mixed_ref, strip_s, send_s, *sems
):
    waves_duo, parts, rows, cols = send_s.shape
    js = strip_s.shape[0]
    duo = strip_s.shape[2] // cols
    ex = make(*sems) if sems else None
    if ex is not None:
        ex.enter()

    def strip(i, _):
        row = pl.multiple_of(i * ROWS, ROWS)
        widths = strip_widths(levels_ref, offsets_ref, row)

        def body(r, lanes, y):
            hidden = (y * jnp.tanh(y) + y).astype(jnp.bfloat16)
            strip_s[:, r, lanes] = dot(out_w_ref[...], hidden)[:js] + out_b_ref[...]

        each_chunk(widths, slope_ref, bias_ref, body)
        for block in range(waves_duo):
            wave, d = block // duo, block % duo
            for part in range(parts):
                piece = strip_s[wave * parts + part, :, d * cols : (d + 1) * cols].astype(jnp.bfloat16)
                send_s[block, part, pl.ds(row, ROWS), :] = piece
        return 0

    strips = rows // ROWS
    if ex is None:
        lax.fori_loop(0, strips, strip, 0)
        out_ref[...] = send_s[...]
    else:
        for piece in range(PIECES):
            lax.fori_loop(piece * strips // PIECES, (piece + 1) * strips // PIECES, strip, 0)
            send_piece(ex, send_s, out_ref, piece, rows // PIECES, True)
    mixed_strips(levels_ref, offsets_ref, slope_ref, bias_ref, back_w_ref, mixed_ref, strip_s, 0)
    if ex is not None:
        for piece in range(PIECES):
            send_piece(ex, send_s, out_ref, piece, rows // PIECES, False)


def gradient_kernel(*refs):
    mixed_refs, cot_ref, grad_ref = refs[:-2], refs[-2], refs[-1]
    blocks, parts, rows, cols = cot_ref.shape
    duo = grad_ref.shape[1] // cols
    base = 0
    for mixed_ref in mixed_refs:
        here = mixed_ref.shape[1]

        def strip(i, _, mixed_ref=mixed_ref, base=base):
            own = pl.ds(pl.multiple_of(i * ROWS, ROWS), ROWS)
            at = pl.ds(pl.multiple_of(base + i * ROWS, ROWS), ROWS)
            for d in range(duo):
                lanes = slice(d * cols, (d + 1) * cols)
                total = jnp.zeros((ROWS, cols), jnp.float32)
                for block in range(d, blocks, duo):
                    for part in range(parts):
                        j = block // duo * parts + part
                        total = total + mixed_ref[j, own, lanes] * cot_ref[block, part, at, :].astype(jnp.float32)
                grad_ref[at, lanes] = total
            return 0

        lax.fori_loop(0, here // ROWS, strip, 0)
        base += here


def unit_tables(w_in, b_in, w_out, b_out, waves, lane):
    units, js = w_out.shape
    spread = lambda x: jnp.broadcast_to((0.5 * x)[:, None], (units, lane))
    ordered = w_out.reshape(units, 2, waves).transpose(2, 1, 0).reshape(js, units)
    out_w = jnp.zeros((max(16, js), units), jnp.bfloat16).at[:js].set(ordered)
    out_b = b_out.reshape(2, waves).T.reshape(js, 1)
    high, low = halves(ordered.astype(jnp.float32) * (0.5 * w_in)[None, :])
    return spread(w_in), spread(b_in), jnp.concatenate([high, low]), out_w, out_b


def col_forward_chunks(load, tw_ref, hi_s, lo_s):
    points, cols = hi_s.shape[1] // 2, hi_s.shape[2]
    lane = tw_ref.shape[3]

    def chunk(i, _):
        row = pl.multiple_of(i * ROWS, ROWS)
        at = pl.ds(row, ROWS)
        at_im = pl.ds(pl.multiple_of(points + row, ROWS), ROWS)
        for c in range(cols // lane):
            lanes = slice(c * lane, (c + 1) * lane)
            out = dft8([load(n, at, lanes) for n in range(RADIX)], -1)
            for k in range(RADIX):
                pair = out[k] if k == 0 else mul(out[k], (tw_ref[0, k, at, :], tw_ref[1, k, at, :]))
                hi_s[k, at, lanes], lo_s[k, at, lanes] = halves(pair[0])
                hi_s[k, at_im, lanes], lo_s[k, at_im, lanes] = halves(pair[1])
        return 0

    lax.fori_loop(0, points // ROWS, chunk, 0)


def col_forward_dots(fh_ref, fl_ref, hi_s, lo_s, out_ref, send_s, ex, beside):
    def fill(k):
        high = hi_s[k]
        y = dot(fh_ref[...], high) + dot(fh_ref[...], lo_s[k]) + dot(fl_ref[...], high)
        put_block(send_s, k, y)

    blocks_out(ex, send_s, out_ref, fill, beside)


def col_inverse_dots(in_ref, gh_ref, gl_ref, tw_ref, mid_s):
    points, cols = mid_s.shape[2], mid_s.shape[3]
    lane = tw_ref.shape[3]
    scale = 1.0 / (RADIX * points)

    def step(k, _):
        high, low = halves(as_float(in_ref[k, : 2 * points]))
        z = dot(gh_ref[...], high) + dot(gh_ref[...], low) + dot(gl_ref[...], high)
        sent = block_scale(in_ref, k)
        z = z * (scale if sent is None else sent[:1] * scale)
        for c in range(cols // lane):
            lanes = slice(c * lane, (c + 1) * lane)
            pair = mul_conj((z[:points, lanes], z[points:, lanes]), (tw_ref[0, k], tw_ref[1, k]))
            mid_s[k, 0, :, lanes] = pair[0]
            mid_s[k, 1, :, lanes] = pair[1]
        return 0

    lax.fori_loop(0, RADIX, step, 0)


def first_kernel(make, t_ref, tw_ref, fh_ref, fl_ref, out_ref, kern_ref, hi_s, lo_s, send_s, *sems):
    ex = make(*sems) if sems else None
    if ex is not None:
        ex.enter()

    def load(n, at, lanes):
        return (t_ref[n, 0, at, lanes].astype(jnp.float32), t_ref[n, 1, at, lanes].astype(jnp.float32))

    col_forward_chunks(load, tw_ref, hi_s, lo_s)
    col_forward_dots(fh_ref, fl_ref, hi_s, lo_s, out_ref, send_s, ex, lambda: transfer_rows(kern_ref))
    if ex is None:
        out_ref[...] = send_s[...]


def focus_kernel(
    make, level, waves, first, in_ref, tw_ref, fh_ref, fl_ref, gh_ref, gl_ref, rowsel_ref, colsel_ref,
    levels_ref, offsets_ref, slope_ref, bias_ref, back_w_ref,
    out_ref, mixed_ref, hi_s, lo_s, mid_s, spot_s, strip_s, send_s, *sems
):
    points, cols = mid_s.shape[2], mid_s.shape[3]
    lane = tw_ref.shape[3]
    ex = make(*sems) if sems else None
    if ex is not None:
        ex.enter()
    col_inverse_dots(in_ref, gh_ref, gl_ref, tw_ref, mid_s)
    for n in range(RADIX):
        spot_s[n] = dot(rowsel_ref[n], colsel_ref[...]) * level

    def chunk(i, _):
        at = pl.ds(pl.multiple_of(i * ROWS, ROWS), ROWS)
        for c in range(cols // lane):
            lanes = slice(c * lane, (c + 1) * lane)
            out = dft8([(mid_s[k, 0, at, lanes], mid_s[k, 1, at, lanes]) for k in range(RADIX)], 1)
            for n in range(RADIX):
                re, im = out[n]
                weight = (re * re + im * im - spot_s[n, at, lanes]) * (1.0 / waves)
                mid_s[n, 0, at, lanes] = weight * re
                mid_s[n, 1, at, lanes] = weight * im
        return 0

    lax.fori_loop(0, points // ROWS, chunk, 0)

    def load(n, at, lanes):
        return (mid_s[n, 0, at, lanes], mid_s[n, 1, at, lanes])

    col_forward_chunks(load, tw_ref, hi_s, lo_s)

    def beside():
        mixed_strips(levels_ref, offsets_ref, slope_ref, bias_ref, back_w_ref, mixed_ref, strip_s, first)

    col_forward_dots(fh_ref, fl_ref, hi_s, lo_s, out_ref, send_s, ex, beside)
    if ex is None:
        out_ref[...] = send_s[...]


def last_kernel(make, in_ref, tw_ref, gh_ref, gl_ref, out_ref, mid_s, send_s, *sems):
    points, cols = mid_s.shape[2], mid_s.shape[3]
    ex = make(*sems) if sems else None
    if ex is not None:
        ex.enter()
    lane = tw_ref.shape[3]
    col_inverse_dots(in_ref, gh_ref, gl_ref, tw_ref, mid_s)

    def chunk(i, _):
        at = pl.ds(pl.multiple_of(i * ROWS, ROWS), ROWS)
        for c in range(cols // lane):
            lanes = slice(c * lane, (c + 1) * lane)
            out = dft8([(mid_s[k, 0, at, lanes], mid_s[k, 1, at, lanes]) for k in range(RADIX)], 1)
            for n in range(RADIX):
                send_s[n, 0, at, lanes] = out[n][0].astype(jnp.bfloat16)
                send_s[n, 1, at, lanes] = out[n][1].astype(jnp.bfloat16)
        return 0

    chunks = points // ROWS
    if ex is None:
        lax.fori_loop(0, chunks, chunk, 0)
        out_ref[...] = send_s[...]
        return
    for piece in range(PIECES):
        lax.fori_loop(piece * chunks // PIECES, (piece + 1) * chunks // PIECES, chunk, 0)
        send_piece(ex, send_s, out_ref, piece, points // PIECES, True)
    for piece in range(PIECES):
        send_piece(ex, send_s, out_ref, piece, points // PIECES, False)


def filter_kernel(
    make, conjugate, first, in_ref, kern_ref, tw_ref, fh_ref, fl_ref, gh_ref, gl_ref,
    levels_ref, offsets_ref, slope_ref, bias_ref, back_w_ref,
    out_ref, mixed_ref, hi_s, lo_s, mid_s, sent_s, strip_s, send_s, *sems
):
    ex = make(*sems) if sems else None
    if ex is not None:
        ex.enter()
    rows, points = mid_s.shape[2], mid_s.shape[3]
    lane = 128
    scale = 1.0 / (RADIX * points)
    coded = in_ref.dtype == jnp.int16
    if coded:
        for n in range(RADIX):
            sent_s[n] = block_scale(in_ref, n)

    def load(n, at, lanes):
        x = as_float(in_ref[n, at, lanes])
        return x * sent_s[n, :, lanes] if coded else x

    def forward(i, _):
        at = pl.ds(pl.multiple_of(i * ROWS, ROWS), ROWS)
        at_im = pl.ds(pl.multiple_of(rows + i * ROWS, ROWS), ROWS)
        for c in range(points // lane):
            lanes = slice(c * lane, (c + 1) * lane)
            lanes_im = slice(points + c * lane, points + (c + 1) * lane)
            out = dft8([(load(n, at, lanes), load(n, at_im, lanes)) for n in range(RADIX)], -1)
            for k in range(RADIX):
                pair = out[k] if k == 0 else mul(out[k], (tw_ref[0, k, :, lanes], tw_ref[1, k, :, lanes]))
                hi_s[k, at, lanes], lo_s[k, at, lanes] = halves(pair[0])
                hi_s[k, at, lanes_im], lo_s[k, at, lanes_im] = halves(pair[1])
        return 0

    lax.fori_loop(0, rows // ROWS, forward, 0)
    combine = mul_conj if conjugate else mul

    def step(k, _):
        high = hi_s[k]
        y = dot(high, gh_ref[...]) + dot(lo_s[k], gh_ref[...]) + dot(high, gl_ref[...])
        re, im = combine((y[:, :points], y[:, points:]), (kern_ref[0, k], kern_ref[1, k]))
        re_h, re_l = halves(re)
        im_h, im_l = halves(im)
        high = jnp.concatenate([re_h, im_h], axis=1)
        low = jnp.concatenate([re_l, im_l], axis=1)
        z = dot(high, fh_ref[...]) + dot(low, fh_ref[...]) + dot(high, fl_ref[...])
        z = z * scale
        t_re, t_im = tw_ref[0, k, 0:1, :], tw_ref[1, k, 0:1, :]
        pair = mul_conj((z[:, :points], z[:, points:]), (t_re, t_im))
        mid_s[k, 0] = pair[0]
        mid_s[k, 1] = pair[1]
        return 0

    lax.fori_loop(0, RADIX, step, 0)

    def inverse(i, _):
        at = pl.ds(pl.multiple_of(i * ROWS, ROWS), ROWS)
        for c in range(points // lane):
            lanes = slice(c * lane, (c + 1) * lane)
            out = dft8([(mid_s[k, 0, at, lanes], mid_s[k, 1, at, lanes]) for k in range(RADIX)], 1)
            for n in range(RADIX):
                mid_s[n, 0, at, lanes], mid_s[n, 1, at, lanes] = out[n]
        return 0

    lax.fori_loop(0, rows // ROWS, inverse, 0)

    def beside():
        mixed_strips(levels_ref, offsets_ref, slope_ref, bias_ref, back_w_ref, mixed_ref, strip_s, first)

    blocks_out(ex, send_s, out_ref, lambda n: put_block(send_s, n, mid_s[n].reshape(2 * rows, points)), beside)
    if ex is None:
        out_ref[...] = send_s[...]


def call(kernel, out_shapes, scratch, name, remote, *args):
    specs = [pl.BlockSpec(memory_space=pltpu.VMEM) for _ in out_shapes]
    more = {}
    make = None
    if remote is not None:
        axes, count, duo, pieces, collective = remote
        specs[0] = pl.BlockSpec(memory_space=pl.ANY)
        scratch = scratch + exchange_scratch(count, pieces)
        more = dict(collective_id=collective, has_side_effects=True)
        make = lambda *sems: Exchange(axes, count, duo, *sems)
    return pl.pallas_call(
        lambda *refs: kernel(make, *refs),
        in_specs=[pl.BlockSpec(memory_space=pltpu.VMEM)] * len(args),
        out_specs=specs,
        out_shape=out_shapes,
        scratch_shapes=scratch,
        compiler_params=params(**more),
        name=name,
    )(*args)


def frequencies(index_all, total_len):
    signed_index = jnp.where(index_all < total_len // 2, index_all, index_all - total_len)
    return signed_index.astype(jnp.float32) * (2.0 * math.pi / total_len)


def transfer_rows(kern_ref):
    rows, points = kern_ref.shape[2], kern_ref.shape[3]
    length = RADIX * points
    focal_length = float(length // 16)
    waves, duo = lax.axis_size("wave"), lax.axis_size("duo")
    own = lax.axis_index("wave") * duo + lax.axis_index("duo")
    wavelength = 1.5 + lax.axis_index("zed").astype(jnp.float32) / (waves - 1)
    wave_number = 2.0 * math.pi / jnp.full((ROWS, 128), wavelength, jnp.float32)

    def chunk(i, _):
        position = own * rows + i * ROWS + lax.broadcasted_iota(jnp.int32, (ROWS, 128), 0)
        kx = frequencies(position // points + RADIX * lax.rem(position, points), length)
        rest = wave_number * wave_number - kx * kx
        at = pl.ds(pl.multiple_of(i * ROWS, ROWS), ROWS)
        for k in range(RADIX):
            for c in range(points // 128):
                v = k + RADIX * (c * 128 + lax.broadcasted_iota(jnp.int32, (ROWS, 128), 1))
                ky = frequencies(v, length)
                kz_square = rest - ky * ky
                kz_root = jnp.sqrt(jnp.abs(kz_square))
                is_open = kz_square > 0.0
                phase_angle = jnp.where(is_open, focal_length * kz_root, 0.0)
                amplitude = jnp.where(is_open, 1.0, jnp.exp(-focal_length * kz_root))
                kern_ref[0, k, at, c * 128 : (c + 1) * 128] = amplitude * jnp.cos(phase_angle)
                kern_ref[1, k, at, c * 128 : (c + 1) * 128] = amplitude * jnp.sin(phase_angle)
        return 0

    lax.fori_loop(0, rows // ROWS, chunk, 0)


def local(levels, offsets, targets, w_in, b_in, w_out, b_out):
    waves, duo = lax.axis_size("wave"), lax.axis_size("duo")
    slabs, group = waves * duo, waves * duo
    rows_here, cols_here = levels.shape
    length = rows_here * slabs
    points = length // RADIX
    cols = cols_here // duo
    rows = length // group
    own = lax.axis_index("wave") * duo + lax.axis_index("duo")
    wave_index = lax.axis_index("zed")

    def exchange(x, axes):
        return lax.all_to_all(x, axes, split_axis=0, concat_axis=0, tiled=True)

    def regroup(x, blocks):
        if x.shape[0] == blocks:
            return x
        flat = x.transpose(1, 0, 2, 3).reshape(2, blocks, -1, x.shape[3])
        return flat.transpose(1, 0, 2, 3)

    def recolumn(x, blocks):
        if x.shape[0] == blocks:
            return x
        flat = x.transpose(1, 2, 0, 3).reshape(2, x.shape[2], blocks, -1)
        return flat.transpose(2, 0, 1, 3)

    fh, fl = dft_block(points)
    gh, gl = fh.T, fl.T
    fh, fl, gh, gl = (jnp.asarray(np.ascontiguousarray(m)) for m in (fh, fl, gh, gl))
    tw = twiddles(points)
    lane = min(128, cols)
    tw_col = jnp.broadcast_to(jnp.asarray(tw)[:, :, :, None], (2, RADIX, points, lane))
    tw_row = jnp.broadcast_to(jnp.asarray(tw)[:, :, None, :], (2, RADIX, ROWS, points))

    own_targets = lax.dynamic_index_in_dim(targets, wave_index, 0, keepdims=False)
    rowsel = (jnp.arange(length, dtype=jnp.int32)[:, None] == own_targets[None, :, 0]).astype(jnp.bfloat16)
    rowsel = rowsel.reshape(RADIX, points, -1)
    colsel = (own_targets[:, 1:2] - own * cols == jnp.arange(cols, dtype=jnp.int32)[None, :]).astype(jnp.bfloat16)

    col_shape = (RADIX, 2, points, cols)
    row_shape = (RADIX, 2, rows, points)
    col_pair = [pltpu.VMEM((RADIX, 2 * points, cols), jnp.bfloat16)] * 2
    row_pair = [pltpu.VMEM((RADIX, rows, 2 * points), jnp.bfloat16)] * 2
    coded = group == RADIX
    wire = jnp.int16 if coded else jnp.float32
    col_send = (RADIX, send_rows(points, coded), cols)
    row_send = (RADIX, send_rows(rows, coded), points)

    def to_rows(x):
        if coded:
            return exchange(x, GROUP)
        return recolumn(exchange(regroup(x.reshape(col_shape), group), GROUP), RADIX).reshape(row_send)

    def to_cols(x):
        if coded:
            return exchange(x, GROUP)
        return regroup(exchange(recolumn(x.reshape(row_shape), group), GROUP), RADIX).reshape(col_send)

    f32, bf16 = jnp.float32, jnp.bfloat16
    strips = rows_here // ROWS
    quarter = strips // 4
    js = 2 * waves
    lane_units = min(256, cols_here)
    slope, bias, back_w, out_w, out_b = unit_tables(w_in, b_in, w_out, b_out, waves, lane_units)
    unit_args = (levels, offsets, slope, bias, back_w)
    strip_s = pltpu.VMEM((js, ROWS, cols_here), f32)

    def mixed_shape(count):
        return jax.ShapeDtypeStruct((js, count * ROWS, cols_here), f32)

    def remote(axes, pieces, collective):
        return (axes, group, duo, pieces, collective) if coded else None

    slab_shape = (slabs, 2, rows_here, cols)
    trans, mixed_a = call(
        surrogate_kernel,
        [jax.ShapeDtypeStruct(slab_shape, bf16), mixed_shape(quarter)],
        [strip_s, pltpu.VMEM(slab_shape, bf16)],
        "surrogate", remote(SLAB, PIECES, 0), *unit_args, out_w, out_b,
    )
    if not coded:
        trans = exchange(trans, SLAB)

    spectrum, kern = call(
        first_kernel,
        [jax.ShapeDtypeStruct(col_send, wire), jax.ShapeDtypeStruct((2, RADIX, rows, points), f32)],
        col_pair + [pltpu.VMEM(col_send, wire)],
        "first", remote(GROUP, 1, 1), regroup(trans, RADIX), tw_col, fh, fl,
    )

    def filtered(spectrum, conjugate, first, collective):
        there = spectrum if coded else to_rows(spectrum)
        done, mixed = call(
            lambda make, *refs: filter_kernel(make, conjugate, first, *refs),
            [jax.ShapeDtypeStruct(row_send, wire), mixed_shape(quarter)],
            row_pair + [pltpu.VMEM(row_shape, f32), pltpu.VMEM((RADIX, ROWS, points), f32), strip_s, pltpu.VMEM(row_send, wire)],
            "filter_back" if conjugate else "filter",
            remote(GROUP, 1, collective),
            there, kern, tw_row, fh, fl, gh, gl, *unit_args,
        )
        return (done if coded else to_cols(done)), mixed

    spectrum, mixed_b = filtered(spectrum, False, quarter, 2)
    spectrum, mixed_c = call(
        lambda make, *refs: focus_kernel(make, float(length // 8), waves, 2 * quarter, *refs),
        [jax.ShapeDtypeStruct(col_send, wire), mixed_shape(quarter)],
        col_pair
        + [pltpu.VMEM(col_shape, f32), pltpu.VMEM((RADIX, points, cols), f32), strip_s, pltpu.VMEM(col_send, wire)],
        "focus", remote(GROUP, 1, 3), spectrum, tw_col, fh, fl, gh, gl, rowsel, colsel, *unit_args,
    )
    spectrum, mixed_d = filtered(spectrum, True, 3 * quarter, 4)
    (cot,) = call(
        last_kernel,
        [jax.ShapeDtypeStruct(col_shape, bf16)],
        [pltpu.VMEM(col_shape, f32), pltpu.VMEM(col_shape, bf16)],
        "last", remote(SLAB, PIECES, 5), spectrum, tw_col, gh, gl,
    )
    if not coded:
        cot = exchange(regroup(cot, slabs), SLAB)
    return pl.pallas_call(
        gradient_kernel,
        out_shape=jax.ShapeDtypeStruct((rows_here, cols_here), f32),
        compiler_params=params(),
        name="gradient",
    )(mixed_a, mixed_b, mixed_c, mixed_d, cot)


def solution(mesh):
    waves, slabs = mesh.shape["wave"], mesh.shape["slab"]
    cut = Mesh(mesh.devices.reshape(waves, waves, slabs // waves), ("wave", "zed", "duo"))
    place = P(("zed", "duo"), "wave")
    placed = (place, place, P(), P(), P(), P(), P())
    return jax.shard_map(local, mesh=cut, in_specs=placed, out_specs=place, check_vma=False)
```
